32 devices in a mesh: groups: 2 (over y), tenant: 4 (over z), out: 2 (over x), inp: 2 (over core).
Axes of the slice: x: 2, y: 2, z: 4, core: 2. Of those that a mesh axis runs over, the one named last changes fastest.
Arguments:
- acts: bfloat16 [2048, 8192], P(('groups', 'tenant'), ('out', 'inp')), parts along dimension 0, may hold values from -6 to 6
- saved_projections: bfloat16 [2048, 2, 14336], P(('groups', 'tenant'), None, ('out', 'inp')), parts along dimension 0, may hold values from -8 to 8
- hidden_gradient: bfloat16 [2048, 14336], P(('groups', 'tenant'), ('out', 'inp')), parts along dimension 0, may hold values from -6 to 6
- adapter_down_weight: bfloat16 [16, 16, 8192], P(('groups', 'tenant'), None, ('out', 'inp')), parts along dimension 0, may hold values from -0.0625 to 0.0625
- adapter_up_weight: bfloat16 [16, 16, 2, 14336], P(('groups', 'tenant'), None, None, ('out', 'inp')), parts along dimension 0, may hold values from -0.0625 to 0.0625
- adapter_per_block: int32 [64], P(('groups', 'tenant')), parts along dimension 0, may hold values from 0 to 7, as said below
Outputs:
- grad_acts: bfloat16 [2048, 8192], P(('groups', 'tenant'), ('out', 'inp')), parts along dimension 0
- grad_a: float32 [16, 16, 8192], P(('groups', 'tenant'), None, ('out', 'inp')), parts along dimension 0
- grad_b: float32 [16, 16, 2, 14336], P(('groups', 'tenant'), None, None, ('out', 'inp')), parts along dimension 0
The draws below stay inside these ranges and needn't reach their ends.
There are 2 independent parts, one for each index of `groups`. The reference program is written for one: setup_inputs(seed, part) draws one part's arguments, and reference() takes and returns one part's arrays. A program takes and returns all parts, laid end to end along the dimension named above; each array names one. Nothing has to cross between parts.
Inputs may be any that keep to these rules, and one draw needn't show every extreme that they name: `adapter_per_block`: adapter a is held by tenant index a // 2. The 8 blocks of one tenant index name adapters of all different holders where there are no more blocks than tenant indices, else every holder at least once; they never name two different adapters held by the same tenant index, but may name one adapter more than once.
All inputs are finite; a program needn't handle non-finite values.
Results may differ from the reference program's by a relative error of at most 0.0058.
Values may be sent and summed in bfloat16 or wider, within the bound.
No kernel may reach another device: no remote copies, remote signals or barrier semaphores. Data moves between devices by JAX's collectives and lax.ppermute only.
A program may use at most 64 MiB of HBM per device.

```python
import jax
import jax.numpy as jnp
from jax import lax

MODEL_WIDTH = 8192
HIDDEN_UNITS = 14336
ADAPTER_RANK = 16
BLOCK = 32
BLK_DEV = 8
ADP_DEV = 2
TOKENS = 1024
BLOCKS = 32
ADAPTER_TOTAL = 8


def draw_adapter_per_block(key, part):
    key = jax.random.fold_in(key, 11)
    owner_count = BLOCKS // BLK_DEV
    distinct = min(BLK_DEV, owner_count)
    keys = jax.random.split(key, 4)
    rank_of = jax.random.permutation(keys[2], owner_count).astype(jnp.int32)
    noise = jax.random.randint(keys[0], (owner_count, owner_count), 0, owner_count).astype(jnp.int32)
    scores = (noise + 2 * (owner_count - rank_of)[None, :]) * owner_count + jnp.arange(owner_count, dtype=jnp.int32)[None, :]
    top_scores, chosen = jax.lax.top_k(scores, distinct)
    spread = jnp.arange(BLK_DEV, dtype=jnp.int32) % distinct
    holder = chosen.astype(jnp.int32)[:, spread]
    local_table = jax.random.randint(keys[3], (owner_count, owner_count), 0, ADP_DEV).astype(jnp.int32)
    local_slot = jnp.take_along_axis(local_table, holder, axis=1)
    return (holder * ADP_DEV + local_slot).reshape(-1).astype(jnp.int32)


def block_scale(stream_key, dims, pieces, smallest, high):
    gain = 1.0
    for dim, blocks in pieces:
        steps = jax.random.uniform(jax.random.fold_in(jax.random.fold_in(stream_key, 6), dim), (blocks,), jnp.float32, smallest / len(pieces), high / len(pieces))
        gain = gain * jnp.repeat(jnp.exp(steps), dims[dim] // blocks).reshape((-1,) + (1,) * (len(dims) - 1 - dim))
    return gain


def gaussian(own_key, shape, scale, bound, shards=(), held_as=jnp.bfloat16):
    array = scale * jax.random.normal(own_key, shape, jnp.float32)
    if shards:
        array = array * block_scale(own_key, shape, shards, -0.22, 0.18)
    return jnp.clip(array, -bound, bound).astype(held_as)


def setup_inputs(seed: int = 0, part: int = 0) -> dict:
    arg_keys = jax.random.split(jax.random.key(seed), 7)
    part_keys = jax.random.split(jax.random.fold_in(arg_keys[6], part), 7)
    return {
        "acts": gaussian(part_keys[0], (TOKENS, MODEL_WIDTH), 1.0, 6.0, ((0, 4), (1, 4))),
        "saved_projections": gaussian(part_keys[1], (TOKENS, 2, HIDDEN_UNITS), 1.5, 8.0, ((0, 4), (2, 4))),
        "hidden_gradient": gaussian(part_keys[2], (TOKENS, HIDDEN_UNITS), 1.0, 6.0, ((0, 4), (1, 4))),
        "adapter_down_weight": gaussian(part_keys[3], (ADAPTER_TOTAL, ADAPTER_RANK, MODEL_WIDTH), MODEL_WIDTH ** -0.5, 0.0625, ((0, 4), (2, 4))),
        "adapter_up_weight": gaussian(part_keys[4], (ADAPTER_TOTAL, ADAPTER_RANK, 2, HIDDEN_UNITS), (HIDDEN_UNITS // 2) ** -0.5, 0.0625, ((0, 4), (3, 4))),
        "adapter_per_block": draw_adapter_per_block(jax.random.fold_in(jax.random.fold_in(arg_keys[6], part), 71), part),
    }


adapter_scale = 2.0


def swiglu_back(saved_projections, hidden_gradient):
    gate_part = saved_projections[:, 0].astype(jnp.float32)
    up_part = saved_projections[:, 1].astype(jnp.float32)
    hidden_grad = hidden_gradient.astype(jnp.float32)
    sigma_gate = jax.nn.sigmoid(gate_part)
    grad_gate = hidden_grad * up_part * sigma_gate * (1.0 + gate_part * (1.0 - sigma_gate))
    grad_up = hidden_grad * gate_part * sigma_gate
    return jnp.stack([grad_gate, grad_up], axis=1).astype(jnp.bfloat16)


def rounded(values):
    narrow = lax.optimization_barrier(values.astype(jnp.bfloat16))
    return narrow.astype(jnp.float32)


def reference(acts, saved_projections, hidden_gradient, adapter_down_weight, adapter_up_weight, adapter_per_block):
    grad_proj = swiglu_back(saved_projections, hidden_gradient)
    owner_count = BLOCKS // BLK_DEV
    act_dev = acts.reshape(owner_count, BLK_DEV, BLOCK, MODEL_WIDTH)
    proj_dev = grad_proj.reshape(owner_count, BLK_DEV, BLOCK, 2, HIDDEN_UNITS)
    ids_dev = adapter_per_block.reshape(owner_count, BLK_DEV)
    lower = jnp.tril(jnp.ones((BLK_DEV, BLK_DEV), jnp.float32), -1)

    def count_per_device(carry, inputs):
        total_a, total_b = carry
        act_blocks, proj_blocks, device_numbers = inputs
        selected_down = adapter_down_weight[device_numbers].astype(jnp.float32)
        selected_up = adapter_up_weight[device_numbers].astype(jnp.float32)
        activation_full = act_blocks.astype(jnp.float32)
        projection_full = proj_blocks.astype(jnp.float32)
        low_in = jnp.einsum("ktd,krd->ktr", activation_full, selected_down)
        low_out = jnp.einsum("ktjf,krjf->ktr", projection_full, selected_up)
        rank_input = rounded(low_in)
        rank_output = rounded(low_out)
        input_gradient = (adapter_scale * jnp.einsum("bmh,bhc->bmc", rank_output, selected_down)).astype(jnp.bfloat16)
        down_portion = adapter_scale * jnp.einsum("mqj,mqh->mhj", activation_full, rank_output)
        up_portion = adapter_scale * jnp.einsum("zly,zlds->zyds", rank_input, projection_full)
        same_adapter = (device_numbers[:, None] == device_numbers[None, :]).astype(jnp.float32)
        merged_a = jnp.einsum("kl,lrd->krd", same_adapter, down_portion, precision=lax.Precision.HIGHEST)
        merged_b = jnp.einsum("kl,lrjf->krjf", same_adapter, up_portion, precision=lax.Precision.HIGHEST)
        first_seen = (jnp.sum(same_adapter * lower, axis=1) == 0).astype(jnp.float32)
        total_a = total_a.at[device_numbers].add(rounded(merged_a) * first_seen[:, None, None])
        total_b = total_b.at[device_numbers].add(rounded(merged_b) * first_seen[:, None, None, None])
        return (total_a, total_b), input_gradient

    start_a = jnp.zeros((ADAPTER_TOTAL, ADAPTER_RANK, MODEL_WIDTH), jnp.float32)
    start_b = jnp.zeros((ADAPTER_TOTAL, ADAPTER_RANK, 2, HIDDEN_UNITS), jnp.float32)
    (grad_a, grad_b), input_gradient = lax.scan(count_per_device, (start_a, start_b), (act_dev, proj_dev, ids_dev))
    return input_gradient.reshape(TOKENS, MODEL_WIDTH), grad_a, grad_b
```

```python
import functools

import jax
import jax.numpy as jnp
from jax import lax
from jax.experimental import pallas as pl
from jax.experimental.pallas import tpu as pltpu
from jax.sharding import PartitionSpec as P

adapter_scale = 2.0
BF = jnp.bfloat16
F32 = jnp.float32
COST = 1


def dot(a, b, ca, cb):
    return lax.dot_general(a, b, (((ca,), (cb,)), ((), ())), preferred_element_type=F32)


def on_chip(body, outs, scratch=(), vmem=16 << 20):
    return pl.pallas_call(
        body,
        out_shape=outs,
        scratch_shapes=list(scratch),
        compiler_params=pltpu.CompilerParams(vmem_limit_bytes=vmem),
        cost_estimate=pl.CostEstimate(flops=COST, bytes_accessed=COST, transcendentals=0),
    )


def asked_slot(ids, slots):
    me = lax.axis_index("tenant")
    return jnp.max(jnp.where(lax.div(ids, slots) == me, lax.rem(ids, slots), 0))


def peer_index(k, count):
    return lax.rem(lax.axis_index("tenant") + k, count)


def choose(count, slots, *refs):
    ids, down, up = refs[:count], refs[count], refs[count + 1]
    outs = refs[count + 2 :]
    for k in range(count):
        asked = asked_slot(ids[k][...], slots)
        outs[k][...] = down[asked]
        outs[count + k][...] = up[asked]


def keep_own(full, row_holder, count, rank):
    total = jnp.zeros((rank, full.shape[1]), F32)
    for k in range(count):
        own = row_holder == peer_index(k, count)
        total = total + jnp.where(own, full[k * rank : (k + 1) * rank], 0.0)
    return total


def rank_in(count, rank, row_holder, acts, *refs):
    down, out, stack = refs[:count], refs[count], refs[count + 1]
    for k in range(count):
        stack[pl.ds(k * rank, rank), :] = down[k][...]
    out[...] = keep_own(dot(stack[...], acts[...], 1, 1), row_holder[...], count, rank)


def rank_out(count, rank, row_holder, gate, up, *refs):
    maps, out, stack = refs[:count], refs[count], refs[count + 1]
    for k in range(count):
        for j in range(2):
            stack[j, pl.ds(k * rank, rank), :] = maps[k][j]
    full = dot(stack[0], gate[...], 1, 1) + dot(stack[1], up[...], 1, 1)
    out[...] = keep_own(full, row_holder[...], count, rank)


def fill_wide(wide, row_holder, low, count, rank):
    narrow = low.astype(BF).astype(F32)
    for k in range(count):
        own = row_holder == peer_index(k, count)
        wide[pl.ds(k * rank, rank), :] = jnp.where(own, narrow, 0.0).astype(BF)


def parts_b(count, rank, row_holder, low, more, gate, up, *refs):
    outs, wide = refs[:count], refs[count]
    fill_wide(wide, row_holder[...], low[...] + more[...], count, rank)
    for j, grad in enumerate((gate, up)):
        part = (adapter_scale * dot(wide[...], grad[...], 1, 0)).astype(BF)
        for k in range(count):
            outs[k][j] = part[k * rank : (k + 1) * rank]


def parts_a(count, rank, row_holder, low, more, acts, *refs):
    outs, wide = refs[:count], refs[count]
    fill_wide(wide, row_holder[...], low[...] + more[...], count, rank)
    part = (adapter_scale * dot(wide[...], acts[...], 1, 0)).astype(BF)
    for k in range(count):
        outs[k][...] = part[k * rank : (k + 1) * rank]


def input_grad(count, rank, row_holder, low, more, *refs):
    down, out, stack, wide = refs[:count], refs[count], refs[count + 1], refs[count + 2]
    fill_wide(wide, row_holder[...], low[...] + more[...], count, rank)
    for k in range(count):
        stack[pl.ds(k * rank, rank), :] = down[k][...]
    out[...] = (adapter_scale * dot(wide[...], stack[...], 0, 0)).astype(BF)


def held_sum_a(count, slots, *refs):
    ids, parts, out = refs[:count], refs[count : 2 * count], refs[2 * count]
    asked = [asked_slot(ids[k][...], slots) for k in range(count)]
    for a in range(slots):
        total = jnp.zeros(parts[0].shape, F32)
        for k in range(count):
            total = total + jnp.where(asked[k] == a, parts[k][...].astype(F32), 0.0)
        out[a] = total


def held_sum_b(count, slots, *refs):
    ids, parts, out = refs[:count], refs[count : 2 * count], refs[2 * count]
    asked = [asked_slot(ids[k][...], slots) for k in range(count)]
    for a in range(slots):
        for j in range(2):
            total = jnp.zeros(parts[0].shape[1:], F32)
            for k in range(count):
                total = total + jnp.where(asked[k] == a, parts[k][j].astype(F32), 0.0)
            out[a, :, j, :] = total


def on_device(acts, saved, hidden, down, up, ids):
    T = lax.axis_size("tenant")
    slots, rank, width = down.shape
    units = up.shape[3]
    rows = acts.shape[0]
    block_rows = rows // ids.shape[0]
    every = range(T)
    shape = jax.ShapeDtypeStruct

    def shift(x, k):
        return lax.ppermute(x, "tenant", [(i, (i + k) % T) for i in range(T)])

    order = sorted(range(1, T), key=lambda k: -min(k, T - k))

    ids_from = {0: ids}
    for k in order:
        ids_from[k] = shift(ids, k)
    ids_from = [ids_from[k].reshape(1, -1) for k in every]

    up_by_gate = jnp.swapaxes(up, 1, 2)
    sends = on_chip(
        functools.partial(choose, T, slots),
        [shape((rank, width), BF)] * T + [shape((2, rank, units), BF)] * T,
    )(*ids_from, down, up_by_gate)
    sends, saved, hidden = lax.optimization_barrier((sends, saved, hidden))
    down_from, up_from = {0: sends[0]}, {0: sends[T]}
    for k in order:
        down_from[k] = shift(sends[k], -k)
    for k in order:
        up_from[k] = shift(sends[T + k], -k)
    down_from = [down_from[k] for k in every]
    up_from = [up_from[k] for k in every]

    saved_by_gate = jnp.swapaxes(saved, 0, 1)
    g = saved_by_gate[0].astype(F32)
    u = saved_by_gate[1].astype(F32)
    h = hidden.astype(F32)
    s = jax.nn.sigmoid(g)
    grad_gate = (h * u * s * (1.0 + g * (1.0 - s))).astype(BF)
    grad_up = (h * g * s).astype(BF)

    row_holder = jnp.repeat(ids // slots, block_rows).reshape(1, rows)

    def feature_sum(x):
        for axis in ("inp", "out"):
            n = lax.axis_size(axis)
            rest = [lax.ppermute(x, axis, [(i, (i + k) % n) for i in range(n)]) for k in range(1, n)]
            more = sum(rest[1:], rest[0]) if rest else jnp.zeros_like(x)
            if axis == "inp":
                x = x + more
        return x, more

    part = functools.partial
    low_in = on_chip(
        part(rank_in, T, rank),
        shape((rank, rows), F32),
        [pltpu.VMEM((T * rank, width), BF)],
    )(row_holder, acts, *down_from)
    low_in, more_in = feature_sum(low_in)
    back_b = on_chip(
        part(parts_b, T, rank),
        [shape((2, rank, units), BF)] * T,
        [pltpu.VMEM((T * rank, rows), BF)],
    )(row_holder, low_in, more_in, grad_gate, grad_up)

    low_out = on_chip(
        part(rank_out, T, rank),
        shape((rank, rows), F32),
        [pltpu.VMEM((2, T * rank, units), BF)],
    )(row_holder, grad_gate, grad_up, *up_from)
    low_out, more_out = feature_sum(low_out)
    back_a = on_chip(
        part(parts_a, T, rank),
        [shape((rank, width), BF)] * T,
        [pltpu.VMEM((T * rank, rows), BF)],
    )(row_holder, low_out, more_out, acts)
    grad_acts = on_chip(
        part(input_grad, T, rank),
        shape((rows, width), BF),
        [pltpu.VMEM((T * rank, width), BF), pltpu.VMEM((T * rank, rows), BF)],
    )(row_holder, low_out, more_out, *down_from)

    got_b = {0: back_b[0]}
    for k in order:
        got_b[k] = shift(back_b[k], k)
    got_a = {0: back_a[0]}
    for k in order:
        got_a[k] = shift(back_a[k], k)
    grad_b = on_chip(
        part(held_sum_b, T, slots),
        shape((slots, rank, 2, units), F32),
    )(*ids_from, *[got_b[k] for k in every])
    grad_a = on_chip(
        part(held_sum_a, T, slots),
        shape((slots, rank, width), F32),
    )(*ids_from, *[got_a[k] for k in every])
    return grad_acts, grad_a, grad_b


def solution(mesh):
    row = ("groups", "tenant")
    col = ("out", "inp")
    return jax.shard_map(
        on_device,
        mesh=mesh,
        in_specs=(
            P(row, col),
            P(row, None, col),
            P(row, col),
            P(row, None, col),
            P(row, None, None, col),
            P(row),
        ),
        out_specs=(
            P(row, col),
            P(row, None, col),
            P(row, None, None, col),
        ),
        check_vma=False,
    )
```

```python
import functools

import jax
import jax.numpy as jnp
from jax import lax
from jax.experimental import pallas as pl
from jax.experimental.pallas import tpu as pltpu
from jax.sharding import PartitionSpec as P

adapter_scale = 2.0
BF = jnp.bfloat16
F32 = jnp.float32
COST = 1


def dot(a, b, ca, cb):
    return lax.dot_general(a, b, (((ca,), (cb,)), ((), ())), preferred_element_type=F32)


def on_chip(body, outs, scratch=(), vmem=16 << 20, **blocks):
    return pl.pallas_call(
        body,
        out_shape=outs,
        scratch_shapes=list(scratch),
        **blocks,
        compiler_params=pltpu.CompilerParams(vmem_limit_bytes=vmem),
        cost_estimate=pl.CostEstimate(flops=COST, bytes_accessed=COST, transcendentals=0),
    )


def asked_slot(ids, slots):
    me = lax.axis_index("tenant")
    return jnp.max(jnp.where(lax.div(ids, slots) == me, lax.rem(ids, slots), 0))


def peer_index(k, count):
    return lax.rem(lax.axis_index("tenant") + k, count)


def bring(ids, down, up, ids_out, down_out, up_out, arrived):
    pairs = ((ids, ids_out), (down, down_out), (up, up_out))
    copies = [pltpu.make_async_copy(a, b, arrived.at[i]) for i, (a, b) in enumerate(pairs)]
    for copy in copies:
        copy.start()
    for copy in copies:
        copy.wait()


def gated_grad(saved, hidden, gate, up):
    g = saved[0].astype(F32)
    u = saved[1].astype(F32)
    h = hidden[...].astype(F32)
    s = jax.nn.sigmoid(g)
    gate[...] = (h * u * s * (1.0 + g * (1.0 - s))).astype(BF)
    up[...] = (h * g * s).astype(BF)


def choose(count, slots, *refs):
    ids, down, up = refs[:count], refs[count], refs[count + 1]
    outs = refs[count + 2 :]
    for k in range(count):
        asked = asked_slot(ids[k][...], slots)
        outs[k][...] = down[asked]
        outs[count + k][...] = up[asked]


def keep_own(full, row_holder, count, rank):
    total = jnp.zeros((rank, full.shape[1]), F32)
    for k in range(count):
        own = row_holder == peer_index(k, count)
        total = total + jnp.where(own, full[k * rank : (k + 1) * rank], 0.0)
    return total


def rank_in(count, rank, row_holder, acts, *refs):
    down, out, stack = refs[:count], refs[count], refs[count + 1]
    for k in range(count):
        stack[pl.ds(k * rank, rank), :] = down[k][...]
    out[...] = keep_own(dot(stack[...], acts[...], 1, 1), row_holder[...], count, rank)


def rank_out(count, rank, row_holder, gate, up, *refs):
    maps, out, stack = refs[:count], refs[count], refs[count + 1]
    for k in range(count):
        for j in range(2):
            stack[j, pl.ds(k * rank, rank), :] = maps[k][j]
    full = dot(stack[0], gate[...], 1, 1) + dot(stack[1], up[...], 1, 1)
    out[...] = keep_own(full, row_holder[...], count, rank)


def fill_wide(wide, row_holder, low, count, rank):
    narrow = low.astype(BF).astype(F32)
    for k in range(count):
        own = row_holder == peer_index(k, count)
        wide[pl.ds(k * rank, rank), :] = jnp.where(own, narrow, 0.0).astype(BF)


def parts_b(count, rank, row_holder, low, more, gate, up, *refs):
    outs, wide = refs[:count], refs[count]
    fill_wide(wide, row_holder[...], low[...] + more[...], count, rank)
    for j, grad in enumerate((gate, up)):
        part = (adapter_scale * dot(wide[...], grad[...], 1, 0)).astype(BF)
        for k in range(count):
            outs[k][j] = part[k * rank : (k + 1) * rank]


def parts_a(count, rank, row_holder, low, more, acts, *refs):
    outs, wide = refs[:count], refs[count]
    fill_wide(wide, row_holder[...], low[...] + more[...], count, rank)
    part = (adapter_scale * dot(wide[...], acts[...], 1, 0)).astype(BF)
    for k in range(count):
        outs[k][...] = part[k * rank : (k + 1) * rank]


def input_grad(count, rank, row_holder, low, more, *refs):
    down, out, stack, wide = refs[:count], refs[count], refs[count + 1], refs[count + 2]
    fill_wide(wide, row_holder[...], low[...] + more[...], count, rank)
    for k in range(count):
        stack[pl.ds(k * rank, rank), :] = down[k][...]
    out[...] = (adapter_scale * dot(wide[...], stack[...], 0, 0)).astype(BF)


def held_sum_a(count, slots, *refs):
    ids, parts, out = refs[:count], refs[count : 2 * count], refs[2 * count]
    asked = [asked_slot(ids[k][...], slots) for k in range(count)]
    for a in range(slots):
        total = jnp.zeros(parts[0].shape, F32)
        for k in range(count):
            total = total + jnp.where(asked[k] == a, parts[k][...].astype(F32), 0.0)
        out[a] = total


def held_sum_b(count, slots, *refs):
    ids, parts, out = refs[:count], refs[count : 2 * count], refs[2 * count]
    asked = [asked_slot(ids[k][...], slots) for k in range(count)]
    for a in range(slots):
        for j in range(2):
            total = jnp.zeros(parts[0].shape[1:], F32)
            for k in range(count):
                total = total + jnp.where(asked[k] == a, parts[k][j].astype(F32), 0.0)
            out[a, :, j, :] = total


def on_device(acts, saved, hidden, down, up, ids):
    T = lax.axis_size("tenant")
    slots, rank, width = down.shape
    units = up.shape[3]
    rows = acts.shape[0]
    block_rows = rows // ids.shape[0]
    every = range(T)
    shape = jax.ShapeDtypeStruct

    def shift(x, k):
        return lax.ppermute(x, "tenant", [(i, (i + k) % T) for i in range(T)])

    order = sorted(range(1, T), key=lambda k: -min(k, T - k))

    ids_from = {0: ids}
    for k in order:
        ids_from[k] = shift(ids, k)
    ids_from = [ids_from[k].reshape(1, -1) for k in every]

    own_ids = ids.reshape(1, -1)
    own_ids, own_down, own_up = on_chip(
        bring,
        [shape(own_ids.shape, ids.dtype), shape(down.shape, BF), shape(up.shape, BF)],
        [pltpu.SemaphoreType.DMA((3,))],
        in_specs=[pl.BlockSpec(memory_space=pl.ANY)] * 3,
    )(own_ids, down, up)
    ids_from[0] = own_ids
    sends = on_chip(
        functools.partial(choose, T, slots),
        [shape((rank, width), BF)] * T + [shape((rank, 2, units), BF)] * T,
    )(*ids_from, own_down, own_up)
    sends, saved, hidden = lax.optimization_barrier((sends, saved, hidden))
    down_from, up_from = {0: sends[0]}, {0: sends[T]}
    for k in order:
        down_from[k] = shift(sends[k], -k)
    for k in order:
        up_from[k] = shift(sends[T + k], -k)
    down_from = [down_from[k] for k in every]
    up_from = [jnp.swapaxes(up_from[k], 0, 1) for k in every]

    saved_by_gate = jnp.swapaxes(saved, 0, 1)
    grad_gate, grad_up = on_chip(
        gated_grad,
        [shape((rows, units), BF)] * 2,
        grid=(8,),
        in_specs=[
            pl.BlockSpec((2, rows // 8, units), lambda i: (0, i, 0)),
            pl.BlockSpec((rows // 8, units), lambda i: (i, 0)),
        ],
        out_specs=[pl.BlockSpec((rows // 8, units), lambda i: (i, 0))] * 2,
    )(saved_by_gate, hidden)

    row_holder = jnp.repeat(ids // slots, block_rows).reshape(1, rows)

    def feature_sum(x):
        for axis in ("inp", "out"):
            n = lax.axis_size(axis)
            rest = [lax.ppermute(x, axis, [(i, (i + k) % n) for i in range(n)]) for k in range(1, n)]
            more = sum(rest[1:], rest[0]) if rest else jnp.zeros_like(x)
            if axis == "inp":
                x = x + more
        return x, more

    part = functools.partial
    down_from, grad_gate, grad_up = lax.optimization_barrier((down_from, grad_gate, grad_up))
    low_in = on_chip(
        part(rank_in, T, rank),
        shape((rank, rows), F32),
        [pltpu.VMEM((T * rank, width), BF)],
    )(row_holder, acts, *down_from)
    low_in, more_in = feature_sum(low_in)
    back_b = on_chip(
        part(parts_b, T, rank),
        [shape((2, rank, units), BF)] * T,
        [pltpu.VMEM((T * rank, rows), BF)],
    )(row_holder, low_in, more_in, grad_gate, grad_up)

    low_out = on_chip(
        part(rank_out, T, rank),
        shape((rank, rows), F32),
        [pltpu.VMEM((2, T * rank, units), BF)],
    )(row_holder, grad_gate, grad_up, *up_from)
    low_out, more_out = feature_sum(low_out)
    back_a = on_chip(
        part(parts_a, T, rank),
        [shape((rank, width), BF)] * T,
        [pltpu.VMEM((T * rank, rows), BF)],
    )(row_holder, low_out, more_out, acts)
    grad_acts = on_chip(
        part(input_grad, T, rank),
        shape((rows, width), BF),
        [pltpu.VMEM((T * rank, width), BF), pltpu.VMEM((T * rank, rows), BF)],
    )(row_holder, low_out, more_out, *down_from)

    got_b = {0: back_b[0]}
    for k in order:
        got_b[k] = shift(back_b[k], k)
    got_a = {0: back_a[0]}
    for k in order:
        got_a[k] = shift(back_a[k], k)
    grad_b = on_chip(
        part(held_sum_b, T, slots),
        shape((slots, rank, 2, units), F32),
    )(*ids_from, *[got_b[k] for k in every])
    grad_a = on_chip(
        part(held_sum_a, T, slots),
        shape((slots, rank, width), F32),
    )(*ids_from, *[got_a[k] for k in every])
    return grad_acts, grad_a, grad_b


def solution(mesh):
    row = ("groups", "tenant")
    col = ("out", "inp")
    return jax.shard_map(
        on_device,
        mesh=mesh,
        in_specs=(
            P(row, col),
            P(row, None, col),
            P(row, col),
            P(row, None, col),
            P(row, None, None, col),
            P(row),
        ),
        out_specs=(
            P(row, col),
            P(row, None, col),
            P(row, None, None, col),
        ),
        check_vma=False,
    )
```

```python
import functools

import jax
import jax.numpy as jnp
from jax import lax
from jax.experimental import pallas as pl
from jax.experimental.pallas import tpu as pltpu
from jax.sharding import PartitionSpec as P

adapter_scale = 2.0
BF = jnp.bfloat16
F32 = jnp.float32
COST = 1


def dot(a, b, ca, cb):
    return lax.dot_general(a, b, (((ca,), (cb,)), ((), ())), preferred_element_type=F32)


def on_chip(body, outs, scratch=(), vmem=16 << 20, **blocks):
    return pl.pallas_call(
        body,
        out_shape=outs,
        scratch_shapes=list(scratch),
        **blocks,
        compiler_params=pltpu.CompilerParams(vmem_limit_bytes=vmem),
        cost_estimate=pl.CostEstimate(flops=COST, bytes_accessed=COST, transcendentals=0),
    )


def steps(count):
    return enumerate(range(count - 1, -1, -1))


def asked_slot(ids, slots):
    me = lax.axis_index("tenant")
    return jnp.max(jnp.where(lax.div(ids, slots) == me, lax.rem(ids, slots), 0))


def peer_index(k, count):
    me = lax.axis_index("tenant")
    return me ^ k if count & (count - 1) == 0 else lax.rem(me + k, count)


def bring(ids, down, up, ids_out, down_out, up_out, arrived):
    pairs = ((ids, ids_out), (down, down_out), (up, up_out))
    copies = [pltpu.make_async_copy(a, b, arrived.at[i]) for i, (a, b) in enumerate(pairs)]
    for copy in copies:
        copy.start()
    for copy in copies:
        copy.wait()


def gated_grad(saved, hidden, gate, up):
    g = saved[0].astype(F32)
    u = saved[1].astype(F32)
    h = hidden[...].astype(F32)
    s = jax.nn.sigmoid(g)
    gate[...] = (h * u * s * (1.0 + g * (1.0 - s))).astype(BF)
    up[...] = (h * g * s).astype(BF)


def choose(count, slots, *refs):
    ids, down, up = refs[:count], refs[count], refs[count + 1]
    outs = refs[count + 2 :]
    for i in range(count):
        asked = asked_slot(ids[i][...], slots)
        outs[i][...] = down[asked]
        outs[count + i][...] = up[asked]


def keep_own(full, row_holder, count, rank):
    total = jnp.zeros((rank, full.shape[1]), F32)
    for i, k in steps(count):
        own = row_holder == peer_index(k, count)
        total = total + jnp.where(own, full[i * rank : (i + 1) * rank], 0.0)
    return total


def rank_in(count, rank, row_holder, acts, *refs):
    down, out, stack = refs[:count], refs[count], refs[count + 1]
    for k in range(count):
        stack[pl.ds(k * rank, rank), :] = down[k][...]
    out[...] = keep_own(dot(stack[...], acts[...], 1, 1), row_holder[...], count, rank)


def rank_out(count, rank, row_holder, gate, up, *refs):
    maps, out, stack = refs[:count], refs[count], refs[count + 1]
    for k in range(count):
        for j in range(2):
            stack[j, pl.ds(k * rank, rank), :] = maps[k][j]
    full = dot(stack[0], gate[...], 1, 1) + dot(stack[1], up[...], 1, 1)
    out[...] = keep_own(full, row_holder[...], count, rank)


def fill_wide(wide, row_holder, low, count, rank):
    narrow = low.astype(BF).astype(F32)
    for i, k in steps(count):
        own = row_holder == peer_index(k, count)
        wide[pl.ds(i * rank, rank), :] = jnp.where(own, narrow, 0.0).astype(BF)


def parts_b(count, rank, row_holder, low, more, gate, up, *refs):
    outs, wide = refs[:count], refs[count]
    fill_wide(wide, row_holder[...], low[...] + more[...], count, rank)
    for j, grad in enumerate((gate, up)):
        part = (adapter_scale * dot(wide[...], grad[...], 1, 0)).astype(BF)
        for k in range(count):
            outs[k][j] = part[k * rank : (k + 1) * rank]


def parts_a(count, rank, row_holder, low, more, acts, *refs):
    outs, wide = refs[:count], refs[count]
    fill_wide(wide, row_holder[...], low[...] + more[...], count, rank)
    part = (adapter_scale * dot(wide[...], acts[...], 1, 0)).astype(BF)
    for k in range(count):
        outs[k][...] = part[k * rank : (k + 1) * rank]


def input_grad(count, rank, row_holder, low, more, *refs):
    down, out, stack, wide = refs[:count], refs[count], refs[count + 1], refs[count + 2]
    fill_wide(wide, row_holder[...], low[...] + more[...], count, rank)
    for k in range(count):
        stack[pl.ds(k * rank, rank), :] = down[k][...]
    out[...] = (adapter_scale * dot(wide[...], stack[...], 0, 0)).astype(BF)


def held_sum_a(count, slots, *refs):
    ids, parts, out = refs[:count], refs[count : 2 * count], refs[2 * count]
    asked = [asked_slot(ids[k][...], slots) for k in range(count)]
    for a in range(slots):
        total = jnp.zeros(parts[0].shape, F32)
        for k in range(count):
            total = total + jnp.where(asked[k] == a, parts[k][...].astype(F32), 0.0)
        out[a] = total


def held_sum_b(count, slots, *refs):
    ids, parts, out = refs[:count], refs[count : 2 * count], refs[2 * count]
    asked = [asked_slot(ids[k][...], slots) for k in range(count)]
    for a in range(slots):
        for j in range(2):
            total = jnp.zeros(parts[0].shape[1:], F32)
            for k in range(count):
                total = total + jnp.where(asked[k] == a, parts[k][j].astype(F32), 0.0)
            out[a, :, j, :] = total


def on_device(acts, saved, hidden, down, up, ids):
    T = lax.axis_size("tenant")
    slots, rank, width = down.shape
    units = up.shape[3]
    rows = acts.shape[0]
    block_rows = rows // ids.shape[0]
    shape = jax.ShapeDtypeStruct

    def shift(x, k):
        if T & (T - 1) == 0:
            return lax.ppermute(x, "tenant", [(i, i ^ abs(k)) for i in range(T)])
        return lax.ppermute(x, "tenant", [(i, (i + k) % T) for i in range(T)])

    order = list(range(T - 1, 0, -1))

    ids_from = {0: ids}
    for k in order:
        ids_from[k] = shift(ids, k)
    ids_from = [ids_from[k].reshape(1, -1) for k in order + [0]]

    own_ids = ids.reshape(1, -1)
    own_ids, own_down, own_up = on_chip(
        bring,
        [shape(own_ids.shape, ids.dtype), shape(down.shape, BF), shape(up.shape, BF)],
        [pltpu.SemaphoreType.DMA((3,))],
        in_specs=[pl.BlockSpec(memory_space=pl.ANY)] * 3,
    )(own_ids, down, up)
    ids_from[-1] = own_ids
    sends = on_chip(
        functools.partial(choose, T, slots),
        [shape((rank, width), BF)] * T + [shape((rank, 2, units), BF)] * T,
    )(*ids_from, own_down, own_up)
    sends, saved, hidden = lax.optimization_barrier((sends, saved, hidden))
    down_from, up_from = {0: sends[T - 1]}, {0: sends[2 * T - 1]}
    for k in order:
        down_from[k] = shift(sends[T - 1 - k], -k)
    for k in order:
        up_from[k] = shift(sends[2 * T - 1 - k], -k)
    down_from = [down_from[k] for k in order + [0]]
    up_from = [jnp.swapaxes(up_from[k], 0, 1) for k in order + [0]]

    saved_by_gate = jnp.swapaxes(saved, 0, 1)
    grad_gate, grad_up = on_chip(
        gated_grad,
        [shape((rows, units), BF)] * 2,
        grid=(8,),
        in_specs=[
            pl.BlockSpec((2, rows // 8, units), lambda i: (0, i, 0)),
            pl.BlockSpec((rows // 8, units), lambda i: (i, 0)),
        ],
        out_specs=[pl.BlockSpec((rows // 8, units), lambda i: (i, 0))] * 2,
    )(saved_by_gate, hidden)

    row_holder = jnp.repeat(ids // slots, block_rows).reshape(1, rows)

    def feature_sum(x):
        for axis in ("inp", "out"):
            n = lax.axis_size(axis)
            rest = [lax.ppermute(x, axis, [(i, (i + k) % n) for i in range(n)]) for k in range(1, n)]
            more = sum(rest[1:], rest[0]) if rest else jnp.zeros_like(x)
            if axis == "inp":
                x = x + more
        return x, more

    part = functools.partial
    down_from, grad_gate, grad_up = lax.optimization_barrier((down_from, grad_gate, grad_up))
    low_in = on_chip(
        part(rank_in, T, rank),
        shape((rank, rows), F32),
        [pltpu.VMEM((T * rank, width), BF)],
    )(row_holder, acts, *down_from)
    low_in, more_in = feature_sum(low_in)
    back_b = on_chip(
        part(parts_b, T, rank),
        [shape((2, rank, units), BF)] * T,
        [pltpu.VMEM((T * rank, rows), BF)],
    )(row_holder, low_in, more_in, grad_gate, grad_up)

    low_out = on_chip(
        part(rank_out, T, rank),
        shape((rank, rows), F32),
        [pltpu.VMEM((2, T * rank, units), BF)],
    )(row_holder, grad_gate, grad_up, *up_from)
    low_out, more_out = feature_sum(low_out)
    back_a = on_chip(
        part(parts_a, T, rank),
        [shape((rank, width), BF)] * T,
        [pltpu.VMEM((T * rank, rows), BF)],
    )(row_holder, low_out, more_out, acts)
    grad_acts = on_chip(
        part(input_grad, T, rank),
        shape((rows, width), BF),
        [pltpu.VMEM((T * rank, width), BF), pltpu.VMEM((T * rank, rows), BF)],
    )(row_holder, low_out, more_out, *down_from)

    got_b = {0: back_b[T - 1]}
    for k in order:
        got_b[k] = shift(back_b[T - 1 - k], k)
    got_a = {0: back_a[T - 1]}
    for k in order:
        got_a[k] = shift(back_a[T - 1 - k], k)
    grad_b = on_chip(
        part(held_sum_b, T, slots),
        shape((slots, rank, 2, units), F32),
    )(*ids_from, *[got_b[k] for k in order + [0]])
    grad_a = on_chip(
        part(held_sum_a, T, slots),
        shape((slots, rank, width), F32),
    )(*ids_from, *[got_a[k] for k in order + [0]])
    return grad_acts, grad_a, grad_b


def solution(mesh):
    row = ("groups", "tenant")
    col = ("out", "inp")
    return jax.shard_map(
        on_device,
        mesh=mesh,
        in_specs=(
            P(row, col),
            P(row, None, col),
            P(row, col),
            P(row, None, col),
            P(row, None, None, col),
            P(row),
        ),
        out_specs=(
            P(row, col),
            P(row, None, col),
            P(row, None, None, col),
        ),
        check_vma=False,
    )
```

```python
import functools

import jax
import jax.numpy as jnp
from jax import lax
from jax.experimental import pallas as pl
from jax.experimental.pallas import tpu as pltpu
from jax.sharding import PartitionSpec as P

adapter_scale = 2.0
BF = jnp.bfloat16
F32 = jnp.float32
COST = 1


def dot(a, b, ca, cb):
    return lax.dot_general(a, b, (((ca,), (cb,)), ((), ())), preferred_element_type=F32)


def on_chip(body, outs, scratch=(), vmem=16 << 20, **blocks):
    return pl.pallas_call(
        body,
        out_shape=outs,
        scratch_shapes=list(scratch),
        **blocks,
        compiler_params=pltpu.CompilerParams(vmem_limit_bytes=vmem),
        cost_estimate=pl.CostEstimate(flops=COST, bytes_accessed=COST, transcendentals=0),
    )


def steps(count):
    return enumerate(range(count - 1, -1, -1))


def asked_slot(ids, slots):
    me = lax.axis_index("tenant")
    return jnp.max(jnp.where(lax.div(ids, slots) == me, lax.rem(ids, slots), 0))


def peer_index(k, count):
    me = lax.axis_index("tenant")
    return me ^ k if count & (count - 1) == 0 else lax.rem(me + k, count)


def bring(ids, down, ids_out, down_out, arrived):
    pairs = ((ids, ids_out), (down, down_out))
    copies = [pltpu.make_async_copy(a, b, arrived.at[i]) for i, (a, b) in enumerate(pairs)]
    for copy in copies:
        copy.start()
    for copy in copies:
        copy.wait()


def gated_grad(saved, hidden, gate, up):
    g = saved[0].astype(F32)
    u = saved[1].astype(F32)
    h = hidden[...].astype(F32)
    s = jax.nn.sigmoid(g)
    gate[...] = (h * u * s * (1.0 + g * (1.0 - s))).astype(BF)
    up[...] = (h * g * s).astype(BF)


def choose(count, slots, *refs):
    ids, down, up = refs[:count], refs[count], refs[count + 1]
    outs = refs[count + 2 :]
    for i in range(count):
        asked = asked_slot(ids[i][...], slots)
        outs[i][...] = down[asked]
        outs[count + i][...] = up[asked]


def keep_own(full, row_holder, count, rank):
    total = jnp.zeros((rank, full.shape[1]), F32)
    for i, k in steps(count):
        own = row_holder == peer_index(k, count)
        total = total + jnp.where(own, full[i * rank : (i + 1) * rank], 0.0)
    return total


def rank_in(count, rank, row_holder, acts, *refs):
    down, out, stack = refs[:count], refs[count], refs[count + 1]
    for k in range(count):
        stack[pl.ds(k * rank, rank), :] = down[k][...]
    out[...] = keep_own(dot(stack[...], acts[...], 1, 1), row_holder[...], count, rank)


def rank_out(count, rank, row_holder, gate, up, *refs):
    maps, out, stack = refs[:count], refs[count], refs[count + 1]
    for k in range(count):
        for j in range(2):
            stack[j, pl.ds(k * rank, rank), :] = maps[k][j]
    full = dot(stack[0], gate[...], 1, 1) + dot(stack[1], up[...], 1, 1)
    out[...] = keep_own(full, row_holder[...], count, rank)


def fill_wide(wide, row_holder, low, count, rank):
    narrow = low.astype(BF).astype(F32)
    for i, k in steps(count):
        own = row_holder == peer_index(k, count)
        wide[pl.ds(i * rank, rank), :] = jnp.where(own, narrow, 0.0).astype(BF)


def parts_b(count, rank, row_holder, low, more, gate, up, *refs):
    outs, wide = refs[:count], refs[count]
    fill_wide(wide, row_holder[...], low[...] + more[...], count, rank)
    for j, grad in enumerate((gate, up)):
        part = (adapter_scale * dot(wide[...], grad[...], 1, 0)).astype(BF)
        for k in range(count):
            outs[k][j] = part[k * rank : (k + 1) * rank]


def parts_a(count, rank, row_holder, low, more, acts, *refs):
    outs, wide = refs[:count], refs[count]
    fill_wide(wide, row_holder[...], low[...] + more[...], count, rank)
    part = (adapter_scale * dot(wide[...], acts[...], 1, 0)).astype(BF)
    for k in range(count):
        outs[k][...] = part[k * rank : (k + 1) * rank]


def input_grad(count, rank, row_holder, low, more, *refs):
    down, out, stack, wide = refs[:count], refs[count], refs[count + 1], refs[count + 2]
    fill_wide(wide, row_holder[...], low[...] + more[...], count, rank)
    for k in range(count):
        stack[pl.ds(k * rank, rank), :] = down[k][...]
    out[...] = (adapter_scale * dot(wide[...], stack[...], 0, 0)).astype(BF)


def asked_weights(count, slots, *refs):
    ids, out = refs[:count], refs[count]
    for k in range(count):
        asked = asked_slot(ids[k][...], slots)
        for a in range(slots):
            out[k, a] = jnp.full(out.shape[2:], (asked == a).astype(F32))


def held_sum_b(count, slots, *refs):
    ids, parts, out = refs[:count], refs[count : 2 * count], refs[2 * count]
    asked = [asked_slot(ids[k][...], slots) for k in range(count)]
    for a in range(slots):
        for j in range(2):
            total = jnp.zeros(parts[0].shape[1:], F32)
            for k in range(count):
                total = total + jnp.where(asked[k] == a, parts[k][j].astype(F32), 0.0)
            out[a, :, j, :] = total


def on_device(acts, saved, hidden, down, up, ids):
    T = lax.axis_size("tenant")
    slots, rank, width = down.shape
    units = up.shape[3]
    rows = acts.shape[0]
    block_rows = rows // ids.shape[0]
    shape = jax.ShapeDtypeStruct

    def shift(x, k):
        if T & (T - 1) == 0:
            return lax.ppermute(x, "tenant", [(i, i ^ abs(k)) for i in range(T)])
        return lax.ppermute(x, "tenant", [(i, (i + k) % T) for i in range(T)])

    order = list(range(T - 1, 0, -1))

    ids_from = {0: ids}
    for k in order:
        ids_from[k] = shift(ids, k)
    ids_from = [ids_from[k].reshape(1, -1) for k in order + [0]]

    own_ids, own_down = on_chip(
        bring,
        [shape((1, ids.shape[0]), ids.dtype), shape(down.shape, BF)],
        [pltpu.SemaphoreType.DMA((2,))],
        in_specs=[pl.BlockSpec(memory_space=pl.ANY)] * 2,
    )(ids.reshape(1, -1), down)
    ids_from[-1] = own_ids
    up_by_gate = jnp.swapaxes(up, 1, 2)
    sends = on_chip(
        functools.partial(choose, T, slots),
        [shape((rank, width), BF)] * T + [shape((2, rank, units), BF)] * T,
    )(*ids_from, own_down, up_by_gate)
    sends, saved, hidden = lax.optimization_barrier((sends, saved, hidden))
    down_from, up_from = {0: sends[T - 1]}, {0: sends[2 * T - 1]}
    for k in order:
        down_from[k] = shift(sends[T - 1 - k], -k)
    for k in order:
        up_from[k] = shift(sends[2 * T - 1 - k], -k)
    down_from = [down_from[k] for k in order + [0]]
    up_from = [up_from[k] for k in order + [0]]

    saved_by_gate = jnp.swapaxes(saved, 0, 1)
    grad_gate, grad_up = on_chip(
        gated_grad,
        [shape((rows, units), BF)] * 2,
        grid=(8,),
        in_specs=[
            pl.BlockSpec((2, rows // 8, units), lambda i: (0, i, 0)),
            pl.BlockSpec((rows // 8, units), lambda i: (i, 0)),
        ],
        out_specs=[pl.BlockSpec((rows // 8, units), lambda i: (i, 0))] * 2,
    )(saved_by_gate, hidden)

    row_holder = jnp.repeat(ids // slots, block_rows).reshape(1, rows)

    def feature_sum(x):
        for axis in ("inp", "out"):
            n = lax.axis_size(axis)
            rest = [lax.ppermute(x, axis, [(i, (i + k) % n) for i in range(n)]) for k in range(1, n)]
            more = sum(rest[1:], rest[0]) if rest else jnp.zeros_like(x)
            if axis == "inp":
                x = x + more
        return x, more

    part = functools.partial
    down_from, grad_gate, grad_up = lax.optimization_barrier((down_from, grad_gate, grad_up))
    low_in = on_chip(
        part(rank_in, T, rank),
        shape((rank, rows), F32),
        [pltpu.VMEM((T * rank, width), BF)],
    )(row_holder, acts, *down_from)
    low_in, more_in = feature_sum(low_in)
    back_b = on_chip(
        part(parts_b, T, rank),
        [shape((2, rank, units), BF)] * T,
        [pltpu.VMEM((T * rank, rows), BF)],
    )(row_holder, low_in, more_in, grad_gate, grad_up)

    low_out = on_chip(
        part(rank_out, T, rank),
        shape((rank, rows), F32),
        [pltpu.VMEM((2, T * rank, units), BF)],
    )(row_holder, grad_gate, grad_up, *up_from)
    low_out, more_out = feature_sum(low_out)
    back_a = on_chip(
        part(parts_a, T, rank),
        [shape((rank, width), BF)] * T,
        [pltpu.VMEM((T * rank, rows), BF)],
    )(row_holder, low_out, more_out, acts)
    grad_acts = on_chip(
        part(input_grad, T, rank),
        shape((rows, width), BF),
        [pltpu.VMEM((T * rank, width), BF), pltpu.VMEM((T * rank, rows), BF)],
    )(row_holder, low_out, more_out, *down_from)

    got_b = {0: back_b[T - 1]}
    for k in order:
        got_b[k] = shift(back_b[T - 1 - k], k)
    got_a = {0: back_a[T - 1]}
    for k in order:
        got_a[k] = shift(back_a[T - 1 - k], k)
    grad_b = on_chip(
        part(held_sum_b, T, slots),
        shape((slots, rank, 2, units), F32),
    )(*ids_from, *[got_b[k] for k in order + [0]])
    weights = on_chip(
        functools.partial(asked_weights, T, slots), shape((T, slots, rank, 1), F32)
    )(*ids_from)
    grad_a = sum(
        weights[i] * got_a[k].astype(F32)[None] for i, k in enumerate(order + [0])
    )
    return grad_acts, grad_a, grad_b


def solution(mesh):
    row = ("groups", "tenant")
    col = ("out", "inp")
    return jax.shard_map(
        on_device,
        mesh=mesh,
        in_specs=(
            P(row, col),
            P(row, None, col),
            P(row, col),
            P(row, None, col),
            P(row, None, None, col),
            P(row),
        ),
        out_specs=(
            P(row, col),
            P(row, None, col),
            P(row, None, None, col),
        ),
        check_vma=False,
    )
```
